32 devices in a mesh: groups: 2 (over x), ctx: 16 (over z, y, core).
Axes of the slice: x: 2, y: 2, z: 4, core: 2. Of those that a mesh axis runs over, the one named last changes fastest.
Arguments:
- layer_normed_input: bfloat16 [4096, 4096], P(('groups', 'ctx')), parts along dimension 0, may hold values from -6 to 6
- queries: bfloat16 [4096, 2048], P(('groups', 'ctx')), parts along dimension 0, may hold values from -300 to 300
- keys: bfloat16 [4096, 512], P(('groups', 'ctx')), parts along dimension 0, may hold values from -4 to 4
- output_gradient: bfloat16 [4096, 2048], P(('groups', 'ctx')), parts along dimension 0, may hold values from -6 to 6
- adapter_down: bfloat16 [4096, 128], replicated, may hold values from -0.09375 to 0.09375
- adapter_up: bfloat16 [128, 512], replicated, may hold values from -0.5 to 0.5
- down_sign_bits: int32 [4096, 32], replicated, may hold values from 0 to 1
- up_sign_bits: int32 [512, 32], replicated, may hold values from 0 to 1
- block_position_order: int32 [64], P('groups'), parts along dimension 0, may hold values from 0 to 31, each once
- document_lengths: int32 [8], P('groups'), parts along dimension 0, may hold values from 1 to 768, 2048 in all
Outputs:
- features: float32 [8, 8192], P('groups'), parts along dimension 0
The draws below stay inside these ranges and needn't reach their ends.
There are 2 independent parts, one for each index of `groups`. The reference program is written for one: setup_inputs(seed, part) draws one part's arguments, and reference() takes and returns one part's arrays. A program takes and returns all parts, laid end to end along the dimension named above; an argument that names none is the same for every part. Nothing has to cross between parts.
Inputs may be any that keep to these rules, and one draw needn't show every extreme that they name: Block of rows k of the pack (rows k * 64 to (k + 1) * 64 - 1) holds positions block_position_order[k] * 64 onward; every block of positions appears once. `document_lengths`: the lengths are positive and sum to 2048; the longest is exactly 768.
All inputs are finite; a program needn't handle non-finite values.
Results may differ from the reference program's by a relative error of at most 0.0038.
Values may be sent and summed in bfloat16 or wider, within the bound.
A program may use at most 64 MiB of HBM per device.

```python
import math
import jax
import jax.numpy as jnp
import numpy as np
from jax import lax

MODEL_WIDTH = 4096
HEAD_SIZE = 128
HEADS = 16
KEY_VALUE_HEADS = 4
ADAPTER_RANK = 128
FEAT_A = 32
FEAT_B = 32
DOCS = 4
GROUP = 4
BLOCK_ROWS = 64
TOKENS = 2048
MOST_DOC = 768
N_CTX = 16


def key_base(key):
    normal_keys = jax.random.normal(key, (TOKENS, KEY_VALUE_HEADS * HEAD_SIZE), jnp.float32)
    return jnp.clip(normal_keys, -4.0, 4.0)


def draw_keys(key, part):
    base = key_base(key)
    return base.astype(jnp.bfloat16)


def draw_queries(key, part):
    key = jax.random.fold_in(key, 5)
    base = jnp.clip(jax.random.normal(key, (TOKENS, HEADS * HEAD_SIZE), jnp.float32), -4.0, 4.0)
    return base.astype(jnp.bfloat16)


def plant(result, stream_key, low, top_value):
    place = [jax.random.randint(jax.random.fold_in(stream_key, axis), (), 0, length) for axis, length in enumerate(result.shape)]
    longest = result.shape.index(max(result.shape))
    next_to = place[:longest] + [(place[longest] + 1) % result.shape[longest]] + place[longest + 1:]
    return result.at[tuple(place)].set(low).at[tuple(next_to)].set(top_value)


def steps_of(own_key, shape, split, smallest, largest):
    gain, own = 1.0, jax.random.fold_in(own_key, 6)
    for position, blocks in split:
        draws = jnp.exp(jax.random.uniform(jax.random.fold_in(own, position), (blocks,), jnp.float32, smallest / len(split), largest / len(split)))
        gain = gain * jnp.repeat(draws, shape[position] // blocks).reshape([-1 if axis == position else 1 for axis in range(len(shape))])
    return gain


def split_up(count, total, reach, skew):
    loads = [(1 << 20) // math.isqrt(standing ** skew) + 1 for standing in range(2, count + 1)]
    spare, given = total - reach - (count - 1), [1] * (count - 1)
    while spare > 0:
        movable = [i for i in range(count - 1) if given[i] < reach]
        whole, left = sum([loads[i] for i in movable]), spare
        for i in movable:
            addition = min(reach - given[i], max(1, left * loads[i] // whole), spare)
            given[i] = given[i] + addition
            spare = spare - addition
    return np.array([reach] + given)


def uneven(rng, number_of, total, bound, lean):
    if number_of == 2:
        one = jax.random.randint(rng, (), max(1, total - bound), min(bound, total - 1) + 1)
        return jnp.stack([one, total - one])
    lengths = jnp.asarray(split_up(number_of, total, bound, lean), jnp.int32)
    pairs = (number_of - 1) // 2
    source_of, receiver = lengths[1:1 + 2 * pairs:2], lengths[2:2 + 2 * pairs:2]
    margin = jnp.minimum(source_of - 1, bound - receiver)
    moved = jax.random.randint(jax.random.fold_in(rng, 1), (pairs,), 0, 1 << 20) % (margin + 1)
    lengths = lengths.at[1:1 + 2 * pairs:2].set(source_of - moved).at[2:2 + 2 * pairs:2].set(receiver + moved)
    return lengths[jax.random.permutation(jax.random.fold_in(rng, 2), number_of)]


def bell_draw(stream_key, dims, scale, bound, split=(), kind=jnp.bfloat16):
    array = jax.random.normal(stream_key, dims, jnp.float32) * scale
    if len(split) > 0:
        array = steps_of(stream_key, dims, split, -0.22, 0.18) * array
    return jnp.clip(array, min=-bound, max=bound).astype(kind)


def setup_inputs(seed: int = 0, part: int = 0) -> dict:
    key_of = jax.random.split(jax.random.key(seed), 11)
    part_splits = jax.random.split(jax.random.fold_in(key_of[10], part), 11)
    return {
        "layer_normed_input": bell_draw(part_splits[0], (TOKENS, MODEL_WIDTH), 1.0, 6.0, ((0, 16),)),
        "queries": draw_queries(jax.random.fold_in(jax.random.fold_in(key_of[10], part), 71), part),
        "keys": draw_keys(jax.random.fold_in(jax.random.fold_in(key_of[10], part), 71), part),
        "output_gradient": bell_draw(part_splits[3], (TOKENS, HEADS * HEAD_SIZE), 1.0, 6.0, ((0, 16),)),
        "adapter_down": bell_draw(key_of[4], (MODEL_WIDTH, ADAPTER_RANK), MODEL_WIDTH ** -0.5, 0.09375),
        "adapter_up": bell_draw(key_of[5], (ADAPTER_RANK, KEY_VALUE_HEADS * HEAD_SIZE), ADAPTER_RANK ** -0.5, 0.5),
        "down_sign_bits": plant(jax.random.randint(key_of[6], (MODEL_WIDTH, FEAT_A), 0, 2), jax.random.fold_in(key_of[6], 1), 0, 1).astype(jnp.int32),
        "up_sign_bits": plant(jax.random.randint(key_of[7], (KEY_VALUE_HEADS * HEAD_SIZE, FEAT_B), 0, 2), jax.random.fold_in(key_of[7], 1), 0, 1).astype(jnp.int32),
        "block_position_order": jax.random.permutation(part_splits[8], 2 * N_CTX).astype(jnp.int32),
        "document_lengths": uneven(part_splits[9], DOCS, TOKENS, MOST_DOC, 2).astype(jnp.int32),
    }


norm_eps = 1e-06
span_cap = 128
far_low = -1e+30

def unit_rows(values):
    return values * lax.rsqrt(lax.optimization_barrier(jnp.mean(values * values, axis=-1, keepdims=True)) + norm_eps)

def reference(layer_normed_input, queries, keys, output_gradient, adapter_down, adapter_up, down_sign_bits, up_sign_bits, block_position_order, document_lengths):
    block_total = TOKENS // BLOCK_ROWS
    row_ids = jnp.arange(TOKENS, dtype=jnp.int32)
    positions = block_position_order[row_ids // BLOCK_ROWS] * BLOCK_ROWS + row_ids % BLOCK_ROWS
    doc_ends = jnp.cumsum(document_lengths).astype(jnp.int32)
    doc_bounds = doc_ends[:DOCS - 1]
    documents = lax.optimization_barrier(jnp.sum((positions[:, None] >= doc_bounds[None, :]).astype(jnp.int32), axis=1))
    doc_starts = (doc_ends - document_lengths).astype(jnp.int32)
    spot_docs = lax.optimization_barrier(jnp.sum((row_ids[:, None] >= doc_bounds[None, :]).astype(jnp.int32), axis=1))
    inverse = jnp.zeros((block_total,), jnp.int32).at[block_position_order].set(jnp.arange(block_total, dtype=jnp.int32))
    storage = inverse[row_ids // BLOCK_ROWS] * BLOCK_ROWS + row_ids % BLOCK_ROWS
    key_span = math.gcd(TOKENS, span_cap)
    ordered_keys = keys[storage].astype(jnp.float32).reshape(TOKENS, KEY_VALUE_HEADS, HEAD_SIZE)
    scale = 1.0 / math.sqrt(HEAD_SIZE)

    def scored(query_heads, query_pos, query_docs, span_index):
        begin = (span_index * key_span).astype(jnp.int32)
        key_block = lax.dynamic_slice_in_dim(ordered_keys, begin, key_span, 0)
        key_pos = begin + jnp.arange(key_span, dtype=jnp.int32)
        key_docs = lax.dynamic_slice_in_dim(spot_docs, begin, key_span)
        allowed = (query_docs[:, None] == key_docs[None, :]) & (key_pos[None, :] <= query_pos[:, None])
        score_block = jnp.einsum('tkgd,ckd->kgtc', query_heads, key_block) * scale
        return (score_block, allowed)

    def block_term(buffer, block_index):
        first = (block_index * BLOCK_ROWS).astype(jnp.int32)
        home = (inverse[block_index] * BLOCK_ROWS).astype(jnp.int32)
        query_heads = lax.dynamic_slice_in_dim(queries, home, BLOCK_ROWS, 0).astype(jnp.float32)
        query_heads = query_heads.reshape(BLOCK_ROWS, KEY_VALUE_HEADS, GROUP, HEAD_SIZE)
        grad_heads = lax.dynamic_slice_in_dim(output_gradient, home, BLOCK_ROWS, 0).astype(jnp.float32)
        grad_heads = grad_heads.reshape(BLOCK_ROWS, KEY_VALUE_HEADS, GROUP, HEAD_SIZE)
        query_pos = first + jnp.arange(BLOCK_ROWS, dtype=jnp.int32)
        query_docs = lax.dynamic_slice_in_dim(spot_docs, first, BLOCK_ROWS)
        first_span = (doc_starts[query_docs[0]] // key_span).astype(jnp.int32)
        end_span = ((first + BLOCK_ROWS - 1) // key_span + 1).astype(jnp.int32)

        def gather_stats(span_index, stat_carry):
            running_top, running_sum = stat_carry
            score_block, allowed = scored(query_heads, query_pos, query_docs, span_index)
            new_top = jnp.maximum(running_top, lax.optimization_barrier(jnp.max(jnp.where(allowed, score_block, -jnp.inf), axis=-1)))
            fresh_sum = lax.optimization_barrier(jnp.sum(jnp.where(allowed, jnp.exp(score_block - new_top[..., None]), 0.0), axis=-1))
            return (new_top, running_sum * jnp.exp(running_top - new_top) + fresh_sum)
        initial = (jnp.full((KEY_VALUE_HEADS, GROUP, BLOCK_ROWS), far_low, jnp.float32), jnp.zeros((KEY_VALUE_HEADS, GROUP, BLOCK_ROWS), jnp.float32))
        running_top, running_sum = lax.fori_loop(first_span, end_span, gather_stats, initial)
        log_total = running_top + jnp.log(running_sum)

        def add_values(span_index, accum):
            score_block, allowed = scored(query_heads, query_pos, query_docs, span_index)
            weights = jnp.where(allowed, jnp.exp(score_block - log_total[..., None]), 0.0)
            weights = lax.optimization_barrier(weights.astype(jnp.bfloat16)).astype(jnp.float32)
            addend = jnp.einsum('kgtc,tkgd->ckd', weights, grad_heads)
            begin = (span_index * key_span).astype(jnp.int32)
            current = lax.dynamic_slice_in_dim(accum, begin, key_span, 0)
            return lax.dynamic_update_slice_in_dim(accum, current + addend, begin, 0)
        return lax.fori_loop(first_span, end_span, add_values, buffer)

    def shard_step(accum, shard):
        buffer = jnp.zeros((TOKENS, KEY_VALUE_HEADS, HEAD_SIZE), jnp.float32)
        buffer = block_term(buffer, block_position_order[2 * shard])
        buffer = block_term(buffer, block_position_order[2 * shard + 1])
        return (accum + buffer, None)
    value_total, ignored = lax.scan(shard_step, jnp.zeros((TOKENS, KEY_VALUE_HEADS, HEAD_SIZE), jnp.float32), jnp.arange(N_CTX, dtype=jnp.int32))
    value_gradient_sum = value_total.reshape(TOKENS, KEY_VALUE_HEADS * HEAD_SIZE)[positions]
    low_rank_term = jnp.dot(layer_normed_input, adapter_down, preferred_element_type=jnp.float32).astype(jnp.bfloat16)
    backward_step = lax.dot_general(value_gradient_sum, adapter_up.astype(jnp.float32), (((1,), (1,)), ((), ())), precision=lax.Precision.HIGHEST)
    member = (documents[:, None] == jnp.arange(DOCS, dtype=jnp.int32)[None, :]).astype(jnp.float32)
    back_docs = (member[:, :, None] * backward_step[:, None, :]).reshape(TOKENS, DOCS * ADAPTER_RANK)
    low_docs = (member[:, :, None] * low_rank_term.astype(jnp.float32)[:, None, :]).reshape(TOKENS, DOCS * ADAPTER_RANK)
    signs_a = (2 * down_sign_bits - 1).astype(jnp.bfloat16)
    signs_b = (2 * up_sign_bits - 1).astype(jnp.float32)
    proj_in = jnp.dot(layer_normed_input, signs_a, preferred_element_type=jnp.float32)
    proj_val = jnp.dot(value_gradient_sum, signs_b, precision=lax.Precision.HIGHEST)
    raw_a = lax.dot_general(proj_in, back_docs, (((0,), (0,)), ((), ())), precision=lax.Precision.HIGHEST)
    raw_b = lax.dot_general(low_docs, proj_val, (((0,), (0,)), ((), ())), precision=lax.Precision.HIGHEST)
    feats_a = raw_a.reshape(FEAT_A, DOCS, ADAPTER_RANK).transpose(1, 0, 2).reshape(DOCS, FEAT_A * ADAPTER_RANK)
    feats_b = raw_b.reshape(DOCS, ADAPTER_RANK * FEAT_B)
    return jnp.concatenate([unit_rows(feats_a), unit_rows(feats_b)], axis=1)
```

```python
import functools
import math

import jax
import jax.numpy as jnp
from jax import lax
from jax.experimental import pallas as pl
from jax.experimental.pallas import tpu as pltpu
from jax.sharding import PartitionSpec as P

HEAD = 128
KV = 4
GROUP = 4
RANK = 128
FEAT = 32
DOCS = 4
BLOCK = 64
ROWS = 128
WIDE = GROUP * ROWS
VROWS = RANK + 2 * FEAT
ACC = VROWS + 16
FAR = -1e30
EPS = 1e-06
GAIN = math.log2(math.e) / math.sqrt(HEAD)
F32 = jnp.float32
BF16 = jnp.bfloat16
NT = (((1,), (1,)), ((), ()))


def split2(x):
    hi = x.astype(BF16)
    return hi, (x - hi.astype(F32)).astype(BF16)


def dot(a, b):
    return jnp.dot(a, b, preferred_element_type=F32)


def dot3(a, b_hi, b_lo):
    hi, lo = split2(a)
    return dot(hi, b_hi) + dot(lo, b_hi) + dot(hi, b_lo)


def kernel(
    n_dev,
    x_hbm, q_hbm, k_hbm, g_hbm, ad_hbm, au_hbm, ds_hbm, us_hbm, order, lengths,
    out_ref,
    x_v, q_v, k_v, g_v, ad_v, au_v, ds_v, us_v,
    kbuf, vbuf, qs, w_hi, w_lo, m_ref, acc, lr_t, partial, rbuf, fin, doc_rows,
    in_sem, ring_send, ring_recv, sib_send, sib_recv, ar_send, ar_recv,
):
    n = n_dev // 2
    half = n // 2
    me = lax.axis_index("ctx")
    core = lax.rem(me, 2)
    chip = me // 2
    fold = lax.rem(chip, 2)
    spot = (chip // 2) * (1 - 2 * fold) + fold * (n - 1)

    def device_at(place, which):
        side = place // half
        return 2 * (2 * (place * (1 - 2 * side) + side * (n - 1)) + side) + which

    ahead = device_at(lax.rem(spot + 1, n), core)
    behind = device_at(lax.rem(spot + n - 1, n), core)
    sibling = 2 * chip + 1 - core

    loads = [
        pltpu.make_async_copy(src, dst, in_sem.at[i])
        for i, (src, dst) in enumerate(
            [(k_hbm, k_v), (x_hbm, x_v), (ad_hbm, ad_v), (ds_hbm, ds_v),
             (q_hbm, q_v), (g_hbm, g_v), (au_hbm, au_v), (us_hbm, us_v)]
        )
    ]
    for load in loads:
        load.start()

    def part(slot, which, m):
        if m < 2:
            return kbuf.at[slot, pl.ds(2 * m, 2), which]
        return vbuf.at[slot, pl.ds((VROWS // 2) * (m - 2), VROWS // 2), pl.ds(ROWS * which, ROWS)]

    def ring(way, step, m):
        src, dst = (step, step + 1) if way == 0 else ((n - step) % n, n - step - 1)
        return pltpu.make_async_remote_copy(
            src_ref=part(src, 0, m), dst_ref=part(dst, 0, m),
            send_sem=ring_send.at[way, step, m], recv_sem=ring_recv.at[dst, m],
            device_id={"ctx": ahead if way == 0 else behind},
            device_id_type=pl.DeviceIdType.MESH,
        )

    def across(slot, m):
        return pltpu.make_async_remote_copy(
            src_ref=part(slot, 0, m), dst_ref=part(slot, 1, m),
            send_sem=sib_send.at[slot, m], recv_sem=sib_recv.at[slot, m],
            device_id={"ctx": sibling}, device_id_type=pl.DeviceIdType.MESH,
        )

    sent = []

    def launch(copy):
        copy.start()
        sent.append(copy)

    barrier = pltpu.get_barrier_semaphore()
    for peer in (ahead, behind, sibling):
        pl.semaphore_signal(
            barrier, inc=1, device_id={"ctx": peer}, device_id_type=pl.DeviceIdType.MESH
        )
    loads[0].wait()
    for g in range(KV):
        kbuf[0, g, 0] = k_v[:, g * HEAD:(g + 1) * HEAD]
    pl.semaphore_wait(barrier, 3)
    for m in (0, 1):
        launch(ring(0, 0, m))
        launch(ring(1, 0, m))
        launch(across(0, m))

    for load in loads[1:4]:
        load.wait()
    low = dot(x_v[...], ad_v[...])
    signs_a = (2 * ds_v[...] - 1).astype(F32).astype(BF16)
    proj = dot(x_v[...], signs_a)
    lr_t[...] = low.T
    proj_hi, proj_lo = split2(proj.T)
    for k in range(4):
        vbuf[0, k * 32:(k + 1) * 32, 0:ROWS] = lr_t[pl.ds(k, 32, stride=4), :].astype(BF16)
    vbuf[0, RANK:RANK + FEAT, 0:ROWS] = proj_hi
    vbuf[0, RANK + FEAT:VROWS, 0:ROWS] = proj_lo
    for m in (2, 3):
        launch(ring(0, 0, m))
        launch(ring(1, 0, m))
        launch(across(0, m))

    tail_row = lax.broadcasted_iota(jnp.int32, (16, 2 * ROWS), 0)
    ones = jnp.where(tail_row == 0, 1.0, 0.0).astype(BF16)
    for s in range(n):
        vbuf[s, VROWS:ACC, :] = ones
    m_ref[...] = jnp.full(m_ref.shape, FAR, F32)
    acc[...] = jnp.zeros(acc.shape, F32)

    end0 = lengths[0]
    end1 = end0 + lengths[1]
    end2 = end1 + lengths[2]

    def positions(first, second, index):
        return jnp.where(index < BLOCK, first * BLOCK + index, second * BLOCK + index - BLOCK)

    def document(pos):
        return (
            (pos >= end0).astype(jnp.int32)
            + (pos >= end1).astype(jnp.int32)
            + (pos >= end2).astype(jnp.int32)
        )

    here0, here1 = order[2 * me], order[2 * me + 1]
    down = lax.broadcasted_iota(jnp.int32, (ROWS, ROWS), 0)
    along = lax.broadcasted_iota(jnp.int32, (ROWS, ROWS), 1)
    doc_down = document(positions(here0, here1, down))
    pos_along = positions(here0, here1, along)
    doc_along = document(pos_along)
    low_along = jnp.where(
        doc_along == 0, 0, jnp.where(doc_along == 1, end0, jnp.where(doc_along == 2, end1, end2))
    )
    member_b = jnp.where(doc_down == along // FEAT, 1.0, 0.0)
    member_a = jnp.where(doc_along == down // FEAT, 1.0, 0.0)
    doc_rows[...] = member_a

    for load in loads[4:]:
        load.wait()
    for g in range(KV):
        for h in range(GROUP):
            lane = (g * GROUP + h) * HEAD
            qs[g, h * ROWS:(h + 1) * ROWS, :] = q_v[:, lane:lane + HEAD]
    signs_b = (2 * us_v[...] - 1).astype(F32).astype(BF16)
    signs_b = jnp.concatenate([signs_b] * DOCS, axis=1)
    for g in range(KV):
        up_g = au_v[:, g * HEAD:(g + 1) * HEAD]
        sign_g = signs_b[g * HEAD:(g + 1) * HEAD, :]
        for h in range(GROUP):
            lane = (g * GROUP + h) * HEAD
            grad = g_v[:, lane:lane + HEAD]
            rows = slice(h * ROWS, (h + 1) * ROWS)
            a_hi, a_lo = split2(lax.dot_general(grad, up_g, NT, preferred_element_type=F32))
            b_hi, b_lo = split2(dot(grad, sign_g) * member_b)
            w_hi[g, rows, 0:RANK] = a_hi
            w_lo[g, rows, 0:RANK] = a_lo
            w_hi[g, rows, RANK:2 * RANK] = b_hi
            w_lo[g, rows, RANK:2 * RANK] = b_lo

    def chunk(slot):
        for m in range(4):
            across(slot, m).wait_recv()
        origin = device_at(lax.rem(spot + n - slot, n), 0)
        bias = []
        for which in (0, 1):
            source = origin + core * (1 - 2 * which) + which
            pos = positions(order[2 * source], order[2 * source + 1], down)
            allowed = (pos <= pos_along) & (pos >= low_along)
            bias.append(jnp.where(allowed, 0.0, FAR))
        bias = jnp.concatenate(bias, axis=0)
        bias = jnp.concatenate([bias] * GROUP, axis=1)

        def one(g, carry):
            keys = kbuf[slot, g].reshape(2 * ROWS, HEAD)
            scores = lax.dot_general(keys, qs[g], NT, preferred_element_type=F32) + bias
            before = m_ref[g]
            top = jnp.maximum(before, jnp.max(scores, axis=0, keepdims=True))
            weights = jnp.exp2((scores - top) * GAIN).astype(BF16)
            shrink = jnp.exp2((before - top) * GAIN)
            m_ref[g] = top
            acc[g] = acc[g] * shrink + dot(vbuf[slot], weights)
            return carry

        lax.fori_loop(0, KV, one, 0)

    pending = [0]
    for s in range(1, half):
        work = list(pending)
        for m in range(4):
            for way in (0, 1):
                slot = s if way == 0 else n - s
                ring(way, s - 1, m).wait_recv()
                if s < half - 1 or m % 2 == way:
                    launch(ring(way, s, m))
                launch(across(slot, m))
            if m % 2 == 1 and work:
                chunk(work.pop(0))
        for slot in work:
            chunk(slot)
        pending = [s, n - s]
    chunk(pending[0])
    for m in range(4):
        ring(m % 2, half - 1, m).wait_recv()
        launch(across(half, m))
    chunk(pending[1])
    chunk(half)

    raw_a = jnp.zeros((DOCS * FEAT, RANK), F32)
    raw_b = jnp.zeros((RANK, DOCS * FEAT), F32)
    for g in range(KV):
        scaled = acc[g, 0:VROWS, :] / acc[g, VROWS:VROWS + 1, :]
        left = scaled[RANK:RANK + FEAT] + scaled[RANK + FEAT:VROWS]
        left = jnp.concatenate([left] * DOCS, axis=0)
        left = left * jnp.concatenate([doc_rows[...]] * GROUP, axis=1)
        raw_a = raw_a + dot3(left, w_hi[g, :, 0:RANK], w_lo[g, :, 0:RANK])
        raw_b = raw_b + dot3(
            scaled[0:RANK], w_hi[g, :, RANK:2 * RANK], w_lo[g, :, RANK:2 * RANK]
        )
    partial[0:ROWS, :] = raw_a
    for d in range(DOCS):
        partial[ROWS + d * FEAT:ROWS + (d + 1) * FEAT, :] = jnp.concatenate(
            [raw_b[k * 32:(k + 1) * 32, d * FEAT:(d + 1) * FEAT] for k in range(4)], axis=1
        )

    piece = 2 * ROWS // n_dev

    def rows_of(device):
        return pl.ds(pl.multiple_of(device * piece, piece), piece)

    def scatter(k):
        peer = lax.rem(me + k, n_dev)
        return pltpu.make_async_remote_copy(
            src_ref=partial.at[rows_of(peer)], dst_ref=rbuf.at[k],
            send_sem=ar_send.at[0, k], recv_sem=ar_recv.at[0, k],
            device_id={"ctx": peer}, device_id_type=pl.DeviceIdType.MESH,
        )

    def spread(k):
        peer = lax.rem(me + k, n_dev)
        return pltpu.make_async_remote_copy(
            src_ref=fin.at[me], dst_ref=fin.at[me],
            send_sem=ar_send.at[1, k], recv_sem=ar_recv.at[1, k],
            device_id={"ctx": peer}, device_id_type=pl.DeviceIdType.MESH,
        )

    def arrival(k):
        source = lax.rem(me + n_dev - k, n_dev)
        return pltpu.make_async_remote_copy(
            src_ref=fin.at[source], dst_ref=fin.at[source],
            send_sem=ar_send.at[1, k], recv_sem=ar_recv.at[1, k],
            device_id={"ctx": lax.rem(me + k, n_dev)}, device_id_type=pl.DeviceIdType.MESH,
        )

    for k in range(1, n_dev):
        scatter(k).start()
    rbuf[0] = partial[rows_of(me), :]
    for k in range(1, n_dev):
        scatter(k).wait_recv()
    fin[me] = jnp.sum(rbuf[...], axis=0)
    for k in range(1, n_dev):
        spread(k).start()
    for k in range(1, n_dev):
        arrival(k).wait_recv()
    whole = fin[...].reshape(2 * DOCS, FEAT, RANK)
    mean = jnp.sum(
        jnp.sum(whole * whole, axis=1, keepdims=True), axis=2, keepdims=True
    ) * (1.0 / (FEAT * RANK))
    out_ref[...] = (whole * lax.rsqrt(mean + EPS)).reshape(2 * ROWS, RANK)
    for copy in sent:
        copy.wait_send()
    for k in range(1, n_dev):
        scatter(k).wait_send()
        spread(k).wait_send()


def per_device(n_dev, x, q, k, g, ad, au, ds, us, order, lengths):
    n = n_dev // 2
    anywhere = pl.BlockSpec(memory_space=pl.ANY)
    scalars = pl.BlockSpec(memory_space=pltpu.SMEM)
    dma = pltpu.SemaphoreType.DMA
    vmem = pltpu.VMEM
    out = pl.pallas_call(
        functools.partial(kernel, n_dev),
        out_shape=jax.ShapeDtypeStruct((2 * ROWS, RANK), F32),
        in_specs=[anywhere] * 8 + [scalars] * 2,
        out_specs=pl.BlockSpec(memory_space=pltpu.VMEM),
        scratch_shapes=[vmem(a.shape, a.dtype) for a in (x, q, k, g, ad, au, ds, us)]
        + [
            vmem((n, KV, 2, ROWS, HEAD), BF16),
            vmem((n, ACC, 2 * ROWS), BF16),
            vmem((KV, WIDE, HEAD), BF16),
            vmem((KV, WIDE, 2 * RANK), BF16),
            vmem((KV, WIDE, 2 * RANK), BF16),
            vmem((KV, 1, WIDE), F32),
            vmem((KV, ACC, WIDE), F32),
            vmem((RANK, ROWS), F32),
            vmem((2 * ROWS, RANK), F32),
            vmem((n_dev, 2 * ROWS // n_dev, RANK), F32),
            vmem((n_dev, 2 * ROWS // n_dev, RANK), F32),
            vmem((ROWS, ROWS), F32),
            dma((8,)),
            dma((2, n // 2, 4)),
            dma((n, 4)),
            dma((n, 4)),
            dma((n, 4)),
            dma((2, n_dev)),
            dma((2, n_dev)),
        ],
        compiler_params=pltpu.CompilerParams(
            collective_id=0, has_side_effects=True, vmem_limit_bytes=40 * 1024 * 1024
        ),
    )(x, q, k, g, ad, au, ds, us, order, lengths)
    out = out.reshape(2, DOCS, FEAT * RANK)
    return jnp.concatenate([out[0], out[1]], axis=1)


def solution(mesh):
    rows = P(("groups", "ctx"), None)
    placed = (rows, rows, rows, rows, P(), P(), P(), P(), P("groups"), P("groups"))
    return jax.shard_map(
        functools.partial(per_device, mesh.shape["ctx"]),
        mesh=mesh, in_specs=placed, out_specs=P("groups", None), check_vma=False,
    )
```

```python
import functools
import math

import jax
import jax.numpy as jnp
from jax import lax
from jax.experimental import pallas as pl
from jax.experimental.pallas import tpu as pltpu
from jax.sharding import PartitionSpec as P

HEAD = 128
KV = 4
GROUP = 4
RANK = 128
FEAT = 32
DOCS = 4
BLOCK = 64
ROWS = 128
WIDE = GROUP * ROWS
VROWS = RANK + 2 * FEAT
ACC = VROWS + 16
FAR = -1e30
EPS = 1e-06
GAIN = math.log2(math.e) / math.sqrt(HEAD)
F32 = jnp.float32
BF16 = jnp.bfloat16
NT = (((1,), (1,)), ((), ()))


def split2(x):
    hi = x.astype(BF16)
    return hi, (x - hi.astype(F32)).astype(BF16)


def dot(a, b):
    return jnp.dot(a, b, preferred_element_type=F32)


def dot3(a, b_hi, b_lo):
    hi, lo = split2(a)
    return dot(hi, b_hi) + dot(lo, b_hi) + dot(hi, b_lo)


def kernel(
    n_dev,
    x_hbm, q_hbm, k_hbm, g_hbm, ad_hbm, au_hbm, ds_hbm, us_hbm, order, lengths,
    out_ref,
    x_v, q_v, k_v, g_v, ad_v, au_v, ds_v, us_v,
    kbuf, vbuf, qs, w_hi, w_lo, m_ref, acc, lr_t, partial, rbuf, fin, doc_rows,
    in_sem, ring_send, ring_recv, sib_send, sib_recv, ar_send, ar_recv,
):
    n = n_dev // 2
    half = n // 2
    me = lax.axis_index("ctx")
    core = lax.rem(me, 2)
    chip = me // 2
    fold = lax.rem(chip, 2)
    spot = (chip // 2) * (1 - 2 * fold) + fold * (n - 1)

    def device_at(place, which):
        side = place // half
        return 2 * (2 * (place * (1 - 2 * side) + side * (n - 1)) + side) + which

    ahead = device_at(lax.rem(spot + 1, n), core)
    behind = device_at(lax.rem(spot + n - 1, n), core)
    sibling = 2 * chip + 1 - core

    loads = [
        pltpu.make_async_copy(src, dst, in_sem.at[i])
        for i, (src, dst) in enumerate(
            [(k_hbm, k_v), (x_hbm, x_v), (ad_hbm, ad_v), (ds_hbm, ds_v),
             (q_hbm, q_v), (g_hbm, g_v), (au_hbm, au_v), (us_hbm, us_v)]
        )
    ]
    for load in loads:
        load.start()

    def part(slot, which, m):
        if m < 2:
            return kbuf.at[slot, pl.ds(2 * m, 2), which]
        return vbuf.at[slot, pl.ds((VROWS // 2) * (m - 2), VROWS // 2), pl.ds(ROWS * which, ROWS)]

    def ring(way, step, m):
        src, dst = (step, step + 1) if way == 0 else ((n - step) % n, n - step - 1)
        return pltpu.make_async_remote_copy(
            src_ref=part(src, 0, m), dst_ref=part(dst, 0, m),
            send_sem=ring_send.at[way, step, m], recv_sem=ring_recv.at[dst, m],
            device_id={"ctx": ahead if way == 0 else behind},
            device_id_type=pl.DeviceIdType.MESH,
        )

    def across(slot, m):
        return pltpu.make_async_remote_copy(
            src_ref=part(slot, 0, m), dst_ref=part(slot, 1, m),
            send_sem=sib_send.at[slot, m], recv_sem=sib_recv.at[slot, m],
            device_id={"ctx": sibling}, device_id_type=pl.DeviceIdType.MESH,
        )

    sent = []

    def launch(copy):
        copy.start()
        sent.append(copy)

    barrier = pltpu.get_barrier_semaphore()
    for peer in (ahead, behind, sibling):
        pl.semaphore_signal(
            barrier, inc=1, device_id={"ctx": peer}, device_id_type=pl.DeviceIdType.MESH
        )
    loads[0].wait()
    for g in range(KV):
        kbuf[0, g, 0] = k_v[:, g * HEAD:(g + 1) * HEAD]
    pl.semaphore_wait(barrier, 3)
    for m in (0, 1):
        launch(ring(0, 0, m))
        launch(ring(1, 0, m))
        launch(across(0, m))

    for load in loads[1:4]:
        load.wait()
    low = dot(x_v[...], ad_v[...])
    signs_a = (2 * ds_v[...] - 1).astype(F32).astype(BF16)
    proj = lax.dot_general(signs_a, x_v[...], NT, preferred_element_type=F32)
    lr_t[...] = low.T
    proj_hi, proj_lo = split2(proj)
    for k in range(4):
        vbuf[0, k * 32:(k + 1) * 32, 0:ROWS] = lr_t[pl.ds(k, 32, stride=4), :].astype(BF16)
    vbuf[0, RANK:RANK + FEAT, 0:ROWS] = proj_hi
    vbuf[0, RANK + FEAT:VROWS, 0:ROWS] = proj_lo
    for m in (2, 3):
        launch(ring(0, 0, m))
        launch(ring(1, 0, m))
        launch(across(0, m))

    tail_row = lax.broadcasted_iota(jnp.int32, (16, 2 * ROWS), 0)
    ones = jnp.where(tail_row == 0, 1.0, 0.0).astype(BF16)
    for s in range(n):
        vbuf[s, VROWS:ACC, :] = ones
    m_ref[...] = jnp.full(m_ref.shape, FAR, F32)
    acc[...] = jnp.zeros(acc.shape, F32)

    end0 = lengths[0]
    end1 = end0 + lengths[1]
    end2 = end1 + lengths[2]

    def positions(first, second, index):
        return jnp.where(index < BLOCK, first * BLOCK + index, second * BLOCK + index - BLOCK)

    def document(pos):
        return (
            (pos >= end0).astype(jnp.int32)
            + (pos >= end1).astype(jnp.int32)
            + (pos >= end2).astype(jnp.int32)
        )

    here0, here1 = order[2 * me], order[2 * me + 1]
    down = lax.broadcasted_iota(jnp.int32, (ROWS, ROWS), 0)
    along = lax.broadcasted_iota(jnp.int32, (ROWS, ROWS), 1)
    doc_down = document(positions(here0, here1, down))
    pos_along = positions(here0, here1, along)
    doc_along = document(pos_along)
    low_along = jnp.where(
        doc_along == 0, 0, jnp.where(doc_along == 1, end0, jnp.where(doc_along == 2, end1, end2))
    )
    member_b = jnp.where(doc_down == along // FEAT, 1.0, 0.0)
    member_a = jnp.where(doc_along == down // FEAT, 1.0, 0.0)
    doc_rows[...] = member_a

    for load in loads[4:]:
        load.wait()
    for g in range(KV):
        for h in range(GROUP):
            lane = (g * GROUP + h) * HEAD
            qs[g, h * ROWS:(h + 1) * ROWS, :] = q_v[:, lane:lane + HEAD]
    def weigh():
        signs_b = (2 * us_v[...] - 1).astype(F32).astype(BF16)
        signs_b = jnp.concatenate([signs_b] * DOCS, axis=0)
        for g in range(KV):
            up_g = au_v[:, g * HEAD:(g + 1) * HEAD]
            sign_g = signs_b[:, g * HEAD:(g + 1) * HEAD]
            for h in range(GROUP):
                lane = (g * GROUP + h) * HEAD
                grad = g_v[:, lane:lane + HEAD]
                rows = slice(h * ROWS, (h + 1) * ROWS)
                a_hi, a_lo = split2(lax.dot_general(grad, up_g, NT, preferred_element_type=F32))
                b_hi, b_lo = split2(
                    lax.dot_general(grad, sign_g, NT, preferred_element_type=F32) * member_b
                )
                w_hi[g, rows, 0:RANK] = a_hi
                w_lo[g, rows, 0:RANK] = a_lo
                w_hi[g, rows, RANK:2 * RANK] = b_hi
                w_lo[g, rows, RANK:2 * RANK] = b_lo

    def chunk(*slots):
        biases = []
        for slot in slots:
            for m in range(4):
                across(slot, m).wait_recv()
            origin = device_at(lax.rem(spot + n - slot, n), 0)
            bias = []
            for which in (0, 1):
                source = origin + core * (1 - 2 * which) + which
                pos = positions(order[2 * source], order[2 * source + 1], down)
                allowed = (pos <= pos_along) & (pos >= low_along)
                bias.append(jnp.where(allowed, 0.0, FAR))
            bias = jnp.concatenate(bias, axis=0)
            biases.append(jnp.concatenate([bias] * GROUP, axis=1))

        def one(g, carry):
            before = m_ref[g]
            top = before
            scores = []
            for slot, bias in zip(slots, biases):
                keys = kbuf[slot, g].reshape(2 * ROWS, HEAD)
                part_scores = lax.dot_general(keys, qs[g], NT, preferred_element_type=F32) + bias
                scores.append(part_scores)
                top = jnp.maximum(top, jnp.max(part_scores, axis=0, keepdims=True))
            shrink = jnp.exp2((before - top) * GAIN)
            m_ref[g] = top
            total = acc[g] * shrink
            for slot, part_scores in zip(slots, scores):
                weights = jnp.exp2((part_scores - top) * GAIN).astype(BF16)
                total = total + dot(vbuf[slot], weights)
            acc[g] = total
            return carry

        lax.fori_loop(0, KV, one, 0, unroll=True)

    def pass_on(s, m):
        for way in (0, 1):
            ring(way, s - 1, m).wait_recv()
            if s < half - 1 or m % 2 == way:
                launch(ring(way, s, m))
        for slot in (s, n - s):
            launch(across(slot, m))

    pending = [0]
    for s in range(1, half):
        for m in (0, 1):
            pass_on(s, m)
        chunk(*pending[:1])
        for m in (2, 3):
            pass_on(s, m)
        if s == 1:
            weigh()
        else:
            chunk(*pending[1:])
        pending = [s, n - s]
    for m in range(4):
        ring(m % 2, half - 1, m).wait_recv()
        launch(across(half, m))
    chunk(*pending)
    chunk(half)

    raw_a = jnp.zeros((DOCS * FEAT, RANK), F32)
    raw_b = jnp.zeros((RANK, DOCS * FEAT), F32)
    for g in range(KV):
        scaled = acc[g, 0:VROWS, :] / acc[g, VROWS:VROWS + 1, :]
        left = scaled[RANK:RANK + FEAT] + scaled[RANK + FEAT:VROWS]
        left = jnp.concatenate([left] * DOCS, axis=0)
        left = left * jnp.concatenate([doc_rows[...]] * GROUP, axis=1)
        raw_a = raw_a + dot3(left, w_hi[g, :, 0:RANK], w_lo[g, :, 0:RANK])
        raw_b = raw_b + dot3(
            scaled[0:RANK], w_hi[g, :, RANK:2 * RANK], w_lo[g, :, RANK:2 * RANK]
        )
    partial[0:ROWS, :] = raw_a
    for d in range(DOCS):
        partial[ROWS + d * FEAT:ROWS + (d + 1) * FEAT, :] = jnp.concatenate(
            [raw_b[k * 32:(k + 1) * 32, d * FEAT:(d + 1) * FEAT] for k in range(4)], axis=1
        )

    piece = 2 * ROWS // n_dev

    def rows_of(device):
        return pl.ds(pl.multiple_of(device * piece, piece), piece)

    def scatter(k):
        peer = lax.rem(me + k, n_dev)
        return pltpu.make_async_remote_copy(
            src_ref=partial.at[rows_of(peer)], dst_ref=rbuf.at[k],
            send_sem=ar_send.at[0, k], recv_sem=ar_recv.at[0, k],
            device_id={"ctx": peer}, device_id_type=pl.DeviceIdType.MESH,
        )

    def spread(k):
        peer = lax.rem(me + k, n_dev)
        return pltpu.make_async_remote_copy(
            src_ref=fin.at[me], dst_ref=fin.at[me],
            send_sem=ar_send.at[1, k], recv_sem=ar_recv.at[1, k],
            device_id={"ctx": peer}, device_id_type=pl.DeviceIdType.MESH,
        )

    def arrival(k):
        source = lax.rem(me + n_dev - k, n_dev)
        return pltpu.make_async_remote_copy(
            src_ref=fin.at[source], dst_ref=fin.at[source],
            send_sem=ar_send.at[1, k], recv_sem=ar_recv.at[1, k],
            device_id={"ctx": lax.rem(me + k, n_dev)}, device_id_type=pl.DeviceIdType.MESH,
        )

    for k in range(1, n_dev):
        scatter(k).start()
    rbuf[0] = partial[rows_of(me), :]
    for k in range(1, n_dev):
        scatter(k).wait_recv()
    fin[me] = jnp.sum(rbuf[...], axis=0)
    for k in range(1, n_dev):
        spread(k).start()
    for k in range(1, n_dev):
        arrival(k).wait_recv()
    whole = fin[...].reshape(2 * DOCS, FEAT, RANK)
    mean = jnp.sum(
        jnp.sum(whole * whole, axis=1, keepdims=True), axis=2, keepdims=True
    ) * (1.0 / (FEAT * RANK))
    out_ref[...] = (whole * lax.rsqrt(mean + EPS)).reshape(2 * ROWS, RANK)
    for copy in sent:
        copy.wait_send()
    for k in range(1, n_dev):
        scatter(k).wait_send()
        spread(k).wait_send()


def per_device(n_dev, x, q, k, g, ad, au, ds, us, order, lengths):
    n = n_dev // 2
    ds, us = ds.T, us.T
    anywhere = pl.BlockSpec(memory_space=pl.ANY)
    scalars = pl.BlockSpec(memory_space=pltpu.SMEM)
    dma = pltpu.SemaphoreType.DMA
    vmem = pltpu.VMEM
    out = pl.pallas_call(
        functools.partial(kernel, n_dev),
        out_shape=jax.ShapeDtypeStruct((2 * ROWS, RANK), F32),
        in_specs=[anywhere] * 8 + [scalars] * 2,
        out_specs=pl.BlockSpec(memory_space=pltpu.VMEM),
        scratch_shapes=[vmem(a.shape, a.dtype) for a in (x, q, k, g, ad, au, ds, us)]
        + [
            vmem((n, KV, 2, ROWS, HEAD), BF16),
            vmem((n, ACC, 2 * ROWS), BF16),
            vmem((KV, WIDE, HEAD), BF16),
            vmem((KV, WIDE, 2 * RANK), BF16),
            vmem((KV, WIDE, 2 * RANK), BF16),
            vmem((KV, 1, WIDE), F32),
            vmem((KV, ACC, WIDE), F32),
            vmem((RANK, ROWS), F32),
            vmem((2 * ROWS, RANK), F32),
            vmem((n_dev, 2 * ROWS // n_dev, RANK), F32),
            vmem((n_dev, 2 * ROWS // n_dev, RANK), F32),
            vmem((ROWS, ROWS), F32),
            dma((8,)),
            dma((2, n // 2, 4)),
            dma((n, 4)),
            dma((n, 4)),
            dma((n, 4)),
            dma((2, n_dev)),
            dma((2, n_dev)),
        ],
        compiler_params=pltpu.CompilerParams(
            collective_id=0, has_side_effects=True, vmem_limit_bytes=60 * 1024 * 1024
        ),
    )(x, q, k, g, ad, au, ds, us, order, lengths)
    out = out.reshape(2, DOCS, FEAT * RANK)
    return jnp.concatenate([out[0], out[1]], axis=1)


def solution(mesh):
    rows = P(("groups", "ctx"), None)
    placed = (rows, rows, rows, rows, P(), P(), P(), P(), P("groups"), P("groups"))
    return jax.shard_map(
        functools.partial(per_device, mesh.shape["ctx"]),
        mesh=mesh, in_specs=placed, out_specs=P("groups", None), check_vma=False,
    )
```

```python
import functools
import math

import jax
import jax.numpy as jnp
from jax import lax
from jax.experimental import pallas as pl
from jax.experimental.pallas import tpu as pltpu
from jax.sharding import PartitionSpec as P

HEAD = 128
KV = 4
GROUP = 4
RANK = 128
FEAT = 32
DOCS = 4
BLOCK = 64
ROWS = 128
WIDE = GROUP * ROWS
VROWS = RANK + 2 * FEAT
ACC = VROWS + 16
FAR = -1e30
EPS = 1e-06
GAIN = math.log2(math.e) / math.sqrt(HEAD)
F32 = jnp.float32
BF16 = jnp.bfloat16
NT = (((1,), (1,)), ((), ()))


def split2(x):
    hi = x.astype(BF16)
    return hi, (x - hi.astype(F32)).astype(BF16)


def dot(a, b):
    return jnp.dot(a, b, preferred_element_type=F32)


def dot3(a, b_hi, b_lo):
    hi, lo = split2(a)
    return dot(hi, b_hi) + dot(lo, b_hi) + dot(hi, b_lo)


def kernel(
    n_dev,
    x_hbm, q_hbm, k_hbm, g_hbm, ad_hbm, au_hbm, ds_hbm, us_hbm, order, lengths,
    out_ref,
    x_v, q_v, k_v, g_v, ad_v, au_v, ds_v, us_v,
    kbuf, vbuf, qs, w_hi, w_lo, m_ref, acc, lr_t, partial, rbuf, fin, doc_rows,
    in_sem, ring_send, ring_recv, sib_send, sib_recv, ar_send, ar_recv,
):
    n = n_dev // 2
    half = n // 2
    me = lax.axis_index("ctx")
    core = lax.rem(me, 2)
    chip = me // 2
    fold = lax.rem(chip, 2)
    spot = (chip // 2) * (1 - 2 * fold) + fold * (n - 1)

    def device_at(place, which):
        side = place // half
        return 2 * (2 * (place * (1 - 2 * side) + side * (n - 1)) + side) + which

    ahead = device_at(lax.rem(spot + 1, n), core)
    behind = device_at(lax.rem(spot + n - 1, n), core)
    sibling = 2 * chip + 1 - core

    loads = [
        pltpu.make_async_copy(src, dst, in_sem.at[i])
        for i, (src, dst) in enumerate(
            [(k_hbm, k_v), (x_hbm, x_v), (ad_hbm, ad_v), (ds_hbm, ds_v),
             (q_hbm, q_v), (g_hbm, g_v), (au_hbm, au_v), (us_hbm, us_v)]
        )
    ]
    for load in loads:
        load.start()

    def part(slot, which, m):
        if m < 2:
            return kbuf.at[slot, pl.ds(2 * m, 2), which]
        return vbuf.at[slot, pl.ds((VROWS // 2) * (m - 2), VROWS // 2), pl.ds(ROWS * which, ROWS)]

    def ring(way, step, m):
        src, dst = (step, step + 1) if way == 0 else ((n - step) % n, n - step - 1)
        return pltpu.make_async_remote_copy(
            src_ref=part(src, 0, m), dst_ref=part(dst, 0, m),
            send_sem=ring_send.at[way, step, m], recv_sem=ring_recv.at[dst, m],
            device_id={"ctx": ahead if way == 0 else behind},
            device_id_type=pl.DeviceIdType.MESH,
        )

    def across(slot, m):
        return pltpu.make_async_remote_copy(
            src_ref=part(slot, 0, m), dst_ref=part(slot, 1, m),
            send_sem=sib_send.at[slot, m], recv_sem=sib_recv.at[slot, m],
            device_id={"ctx": sibling}, device_id_type=pl.DeviceIdType.MESH,
        )

    sent = []

    def launch(copy):
        copy.start()
        sent.append(copy)

    barrier = pltpu.get_barrier_semaphore()
    for peer in (ahead, behind, sibling):
        pl.semaphore_signal(
            barrier, inc=1, device_id={"ctx": peer}, device_id_type=pl.DeviceIdType.MESH
        )
    loads[0].wait()
    for g in range(KV):
        kbuf[0, g, 0] = k_v[:, g * HEAD:(g + 1) * HEAD]
    pl.semaphore_wait(barrier, 3)
    for m in (0, 1):
        launch(ring(0, 0, m))
        launch(ring(1, 0, m))
        launch(across(0, m))

    for load in loads[1:4]:
        load.wait()
    low = dot(x_v[...], ad_v[...])
    signs_a = (2 * ds_v[...] - 1).astype(F32).astype(BF16)
    proj = lax.dot_general(signs_a, x_v[...], NT, preferred_element_type=F32)
    lr_t[...] = low.T
    proj_hi, proj_lo = split2(proj)
    for k in range(4):
        vbuf[0, k * 32:(k + 1) * 32, 0:ROWS] = lr_t[pl.ds(k, 32, stride=4), :].astype(BF16)
    vbuf[0, RANK:RANK + FEAT, 0:ROWS] = proj_hi
    vbuf[0, RANK + FEAT:VROWS, 0:ROWS] = proj_lo
    for m in (2, 3):
        launch(ring(0, 0, m))
        launch(ring(1, 0, m))
        launch(across(0, m))

    tail_row = lax.broadcasted_iota(jnp.int32, (16, 2 * ROWS), 0)
    ones = jnp.where(tail_row == 0, 1.0, 0.0).astype(BF16)
    for s in range(n):
        vbuf[s, VROWS:ACC, :] = ones
    m_ref[...] = jnp.full(m_ref.shape, FAR, F32)
    acc[...] = jnp.zeros(acc.shape, F32)

    end0 = lengths[0]
    end1 = end0 + lengths[1]
    end2 = end1 + lengths[2]

    def positions(first, second, index):
        return jnp.where(index < BLOCK, first * BLOCK + index, second * BLOCK + index - BLOCK)

    def document(pos):
        return (
            (pos >= end0).astype(jnp.int32)
            + (pos >= end1).astype(jnp.int32)
            + (pos >= end2).astype(jnp.int32)
        )

    here0, here1 = order[2 * me], order[2 * me + 1]
    down = lax.broadcasted_iota(jnp.int32, (ROWS, ROWS), 0)
    along = lax.broadcasted_iota(jnp.int32, (ROWS, ROWS), 1)
    doc_down = document(positions(here0, here1, down))
    pos_along = positions(here0, here1, along)
    doc_along = document(pos_along)
    low_along = jnp.where(
        doc_along == 0, 0, jnp.where(doc_along == 1, end0, jnp.where(doc_along == 2, end1, end2))
    )
    member_b = jnp.where(doc_down == along // FEAT, 1.0, 0.0)
    member_a = jnp.where(doc_along == down // FEAT, 1.0, 0.0)
    doc_rows[...] = member_a

    for load in loads[4:]:
        load.wait()
    for g in range(KV):
        for h in range(GROUP):
            lane = (g * GROUP + h) * HEAD
            qs[g, h * ROWS:(h + 1) * ROWS, :] = q_v[:, lane:lane + HEAD]
    def weigh():
        signs_b = (2 * us_v[...] - 1).astype(F32).astype(BF16)
        signs_b = jnp.concatenate([signs_b] * DOCS, axis=0)
        for g in range(KV):
            up_g = au_v[:, g * HEAD:(g + 1) * HEAD]
            sign_g = signs_b[:, g * HEAD:(g + 1) * HEAD]
            for h in range(GROUP):
                lane = (g * GROUP + h) * HEAD
                grad = g_v[:, lane:lane + HEAD]
                rows = slice(h * ROWS, (h + 1) * ROWS)
                a_hi, a_lo = split2(lax.dot_general(grad, up_g, NT, preferred_element_type=F32))
                b_hi, b_lo = split2(
                    lax.dot_general(grad, sign_g, NT, preferred_element_type=F32) * member_b
                )
                w_hi[g, rows, 0:RANK] = a_hi
                w_lo[g, rows, 0:RANK] = a_lo
                w_hi[g, rows, RANK:2 * RANK] = b_hi
                w_lo[g, rows, RANK:2 * RANK] = b_lo

    def chunk(*slots):
        biases = []
        for slot in slots:
            for m in range(4):
                across(slot, m).wait_recv()
            origin = device_at(lax.rem(spot + n - slot, n), 0)
            bias = []
            for which in (0, 1):
                source = origin + core * (1 - 2 * which) + which
                pos = positions(order[2 * source], order[2 * source + 1], down)
                allowed = (pos <= pos_along) & (pos >= low_along)
                bias.append(jnp.where(allowed, 0.0, FAR))
            bias = jnp.concatenate(bias, axis=0)
            biases.append(jnp.concatenate([bias] * GROUP, axis=1))

        def one(g, carry):
            before = m_ref[g]
            top = before
            scores = []
            for slot, bias in zip(slots, biases):
                keys = kbuf[slot, g].reshape(2 * ROWS, HEAD)
                part_scores = lax.dot_general(keys, qs[g], NT, preferred_element_type=F32) + bias
                scores.append(part_scores)
                top = jnp.maximum(top, jnp.max(part_scores, axis=0, keepdims=True))
            shrink = jnp.exp2((before - top) * GAIN)
            m_ref[g] = top
            total = acc[g] * shrink
            for slot, part_scores in zip(slots, scores):
                weights = jnp.exp2((part_scores - top) * GAIN).astype(BF16)
                total = total + dot(vbuf[slot], weights)
            acc[g] = total
            return carry

        lax.fori_loop(0, KV, one, 0, unroll=True)

    def pass_on(s, m):
        for way in (0, 1):
            ring(way, s - 1, m).wait_recv()
            if s < half - 1 or m % 2 == way:
                launch(ring(way, s, m))
        for slot in (s, n - s):
            launch(across(slot, m))

    pending = [0]
    for s in range(1, half):
        for m in (0, 1):
            pass_on(s, m)
        for m in (2, 3):
            pass_on(s, m)
        chunk(*pending)
        if s == 1:
            weigh()
        pending = [s, n - s]
    for m in range(4):
        ring(m % 2, half - 1, m).wait_recv()
        launch(across(half, m))
    chunk(*pending)
    chunk(half)

    raw_a = jnp.zeros((DOCS * FEAT, RANK), F32)
    raw_b = jnp.zeros((RANK, DOCS * FEAT), F32)
    for g in range(KV):
        scaled = acc[g, 0:VROWS, :] / acc[g, VROWS:VROWS + 1, :]
        left = scaled[RANK:RANK + FEAT] + scaled[RANK + FEAT:VROWS]
        left = jnp.concatenate([left] * DOCS, axis=0)
        left = left * jnp.concatenate([doc_rows[...]] * GROUP, axis=1)
        raw_a = raw_a + dot3(left, w_hi[g, :, 0:RANK], w_lo[g, :, 0:RANK])
        raw_b = raw_b + dot3(
            scaled[0:RANK], w_hi[g, :, RANK:2 * RANK], w_lo[g, :, RANK:2 * RANK]
        )
    partial[0:ROWS, :] = raw_a
    for d in range(DOCS):
        partial[ROWS + d * FEAT:ROWS + (d + 1) * FEAT, :] = jnp.concatenate(
            [raw_b[k * 32:(k + 1) * 32, d * FEAT:(d + 1) * FEAT] for k in range(4)], axis=1
        )

    piece = 2 * ROWS // n_dev

    def rows_of(device):
        return pl.ds(pl.multiple_of(device * piece, piece), piece)

    def scatter(k):
        peer = lax.rem(me + k, n_dev)
        return pltpu.make_async_remote_copy(
            src_ref=partial.at[rows_of(peer)], dst_ref=rbuf.at[k],
            send_sem=ar_send.at[0, k], recv_sem=ar_recv.at[0, k],
            device_id={"ctx": peer}, device_id_type=pl.DeviceIdType.MESH,
        )

    def spread(k):
        peer = lax.rem(me + k, n_dev)
        return pltpu.make_async_remote_copy(
            src_ref=fin.at[me], dst_ref=fin.at[me],
            send_sem=ar_send.at[1, k], recv_sem=ar_recv.at[1, k],
            device_id={"ctx": peer}, device_id_type=pl.DeviceIdType.MESH,
        )

    def arrival(k):
        source = lax.rem(me + n_dev - k, n_dev)
        return pltpu.make_async_remote_copy(
            src_ref=fin.at[source], dst_ref=fin.at[source],
            send_sem=ar_send.at[1, k], recv_sem=ar_recv.at[1, k],
            device_id={"ctx": lax.rem(me + k, n_dev)}, device_id_type=pl.DeviceIdType.MESH,
        )

    for k in range(1, n_dev):
        scatter(k).start()
    rbuf[0] = partial[rows_of(me), :]
    for copy in sent:
        copy.wait_send()
    for k in range(1, n_dev):
        scatter(k).wait_recv()
    fin[me] = jnp.sum(rbuf[...], axis=0)
    for k in range(1, n_dev):
        spread(k).start()
    for k in range(1, n_dev):
        scatter(k).wait_send()
    for k in range(1, n_dev):
        arrival(k).wait_recv()
    whole = fin[...].reshape(2 * DOCS, FEAT, RANK)
    mean = jnp.sum(
        jnp.sum(whole * whole, axis=1, keepdims=True), axis=2, keepdims=True
    ) * (1.0 / (FEAT * RANK))
    partial[...] = (whole * lax.rsqrt(mean + EPS)).reshape(2 * ROWS, RANK)
    for k in range(2):
        for f in range(FEAT):
            lane = (k * FEAT + f) * RANK
            out_ref[:, lane:lane + RANK] = partial[pl.ds(k * ROWS + f, DOCS, stride=FEAT), :]
    for k in range(1, n_dev):
        spread(k).wait_send()


def per_device(n_dev, x, q, k, g, ad, au, ds, us, order, lengths):
    n = n_dev // 2
    ds, us = ds.T, us.T
    anywhere = pl.BlockSpec(memory_space=pl.ANY)
    scalars = pl.BlockSpec(memory_space=pltpu.SMEM)
    dma = pltpu.SemaphoreType.DMA
    vmem = pltpu.VMEM
    return pl.pallas_call(
        functools.partial(kernel, n_dev),
        out_shape=jax.ShapeDtypeStruct((DOCS, 2 * FEAT * RANK), F32),
        in_specs=[anywhere] * 8 + [scalars] * 2,
        out_specs=pl.BlockSpec(memory_space=pltpu.VMEM),
        scratch_shapes=[vmem(a.shape, a.dtype) for a in (x, q, k, g, ad, au, ds, us)]
        + [
            vmem((n, KV, 2, ROWS, HEAD), BF16),
            vmem((n, ACC, 2 * ROWS), BF16),
            vmem((KV, WIDE, HEAD), BF16),
            vmem((KV, WIDE, 2 * RANK), BF16),
            vmem((KV, WIDE, 2 * RANK), BF16),
            vmem((KV, 1, WIDE), F32),
            vmem((KV, ACC, WIDE), F32),
            vmem((RANK, ROWS), F32),
            vmem((2 * ROWS, RANK), F32),
            vmem((n_dev, 2 * ROWS // n_dev, RANK), F32),
            vmem((n_dev, 2 * ROWS // n_dev, RANK), F32),
            vmem((ROWS, ROWS), F32),
            dma((8,)),
            dma((2, n // 2, 4)),
            dma((n, 4)),
            dma((n, 4)),
            dma((n, 4)),
            dma((2, n_dev)),
            dma((2, n_dev)),
        ],
        compiler_params=pltpu.CompilerParams(
            collective_id=0, has_side_effects=True, vmem_limit_bytes=60 * 1024 * 1024
        ),
    )(x, q, k, g, ad, au, ds, us, order, lengths)


def solution(mesh):
    rows = P(("groups", "ctx"), None)
    placed = (rows, rows, rows, rows, P(), P(), P(), P(), P("groups"), P("groups"))
    return jax.shard_map(
        functools.partial(per_device, mesh.shape["ctx"]),
        mesh=mesh, in_specs=placed, out_specs=P("groups", None), check_vma=False,
    )
```

```python
import functools
import math

import jax
import jax.numpy as jnp
from jax import lax
from jax.experimental import pallas as pl
from jax.experimental.pallas import tpu as pltpu
from jax.sharding import PartitionSpec as P

HEAD = 128
KV = 4
GROUP = 4
RANK = 128
FEAT = 32
DOCS = 4
BLOCK = 64
ROWS = 128
WIDE = GROUP * ROWS
VROWS = RANK + 2 * FEAT
ACC = VROWS + 16
FAR = -1e30
EPS = 1e-06
GAIN = math.log2(math.e) / math.sqrt(HEAD)
F32 = jnp.float32
BF16 = jnp.bfloat16
NT = (((1,), (1,)), ((), ()))


def split2(x):
    hi = x.astype(BF16)
    return hi, (x - hi.astype(F32)).astype(BF16)


def dot(a, b):
    return jnp.dot(a, b, preferred_element_type=F32)


def dot3(a, b_hi, b_lo):
    hi, lo = split2(a)
    both = dot(jnp.concatenate([hi, lo], axis=0), b_hi)
    return both[:a.shape[0]] + both[a.shape[0]:] + dot(hi, b_lo)


def kernel(
    n_dev,
    x_hbm, q_hbm, k_hbm, g_hbm, ad_hbm, au_hbm, ds_hbm, us_hbm, order, lengths,
    out_ref,
    x_v, q_v, k_v, g_v, ad_v, au_v, ds_v, us_v,
    kbuf, vbuf, qs, w_hi, w_lo, m_ref, acc, lr_t, partial, rbuf, fin, doc_rows,
    in_sem, ring_send, ring_recv, sib_send, sib_recv, ar_send, ar_recv,
):
    n = n_dev // 2
    half = n // 2
    me = lax.axis_index("ctx")
    core = lax.rem(me, 2)
    chip = me // 2
    fold = lax.rem(chip, 2)
    spot = (chip // 2) * (1 - 2 * fold) + fold * (n - 1)

    def device_at(place, which):
        side = place // half
        return 2 * (2 * (place * (1 - 2 * side) + side * (n - 1)) + side) + which

    ahead = device_at(lax.rem(spot + 1, n), core)
    behind = device_at(lax.rem(spot + n - 1, n), core)
    sibling = 2 * chip + 1 - core

    loads = [
        pltpu.make_async_copy(src, dst, in_sem.at[i])
        for i, (src, dst) in enumerate(
            [(k_hbm, k_v), (x_hbm, x_v), (ad_hbm, ad_v), (ds_hbm, ds_v),
             (q_hbm, q_v), (g_hbm, g_v), (au_hbm, au_v), (us_hbm, us_v)]
        )
    ]
    for load in loads:
        load.start()

    def part(slot, which, m):
        if m < 2:
            return kbuf.at[slot, pl.ds(2 * m, 2), which]
        return vbuf.at[slot, pl.ds((VROWS // 2) * (m - 2), VROWS // 2), pl.ds(ROWS * which, ROWS)]

    def ring(way, step, m):
        src, dst = (step, step + 1) if way == 0 else ((n - step) % n, n - step - 1)
        return pltpu.make_async_remote_copy(
            src_ref=part(src, 0, m), dst_ref=part(dst, 0, m),
            send_sem=ring_send.at[way, step, m], recv_sem=ring_recv.at[dst, m],
            device_id={"ctx": ahead if way == 0 else behind},
            device_id_type=pl.DeviceIdType.MESH,
        )

    def across(slot, m):
        return pltpu.make_async_remote_copy(
            src_ref=part(slot, 0, m), dst_ref=part(slot, 1, m),
            send_sem=sib_send.at[slot, m], recv_sem=sib_recv.at[slot, m],
            device_id={"ctx": sibling}, device_id_type=pl.DeviceIdType.MESH,
        )

    sent = []

    def launch(copy):
        copy.start()
        sent.append(copy)

    barrier = pltpu.get_barrier_semaphore()
    for peer in (ahead, behind, sibling):
        pl.semaphore_signal(
            barrier, inc=1, device_id={"ctx": peer}, device_id_type=pl.DeviceIdType.MESH
        )
    loads[0].wait()
    for g in range(KV):
        kbuf[0, g, 0] = k_v[:, g * HEAD:(g + 1) * HEAD]
    pl.semaphore_wait(barrier, 3)
    for m in (0, 1):
        launch(ring(0, 0, m))
        launch(ring(1, 0, m))
        launch(across(0, m))

    for load in loads[1:4]:
        load.wait()
    low = dot(x_v[...], ad_v[...])
    signs_a = (2 * ds_v[...] - 1).astype(F32).astype(BF16)
    proj = lax.dot_general(signs_a, x_v[...], NT, preferred_element_type=F32)
    lr_t[...] = low.T
    proj_hi, proj_lo = split2(proj)
    for k in range(4):
        vbuf[0, k * 32:(k + 1) * 32, 0:ROWS] = lr_t[pl.ds(k, 32, stride=4), :].astype(BF16)
    vbuf[0, RANK:RANK + FEAT, 0:ROWS] = proj_hi
    vbuf[0, RANK + FEAT:VROWS, 0:ROWS] = proj_lo
    for m in (2, 3):
        launch(ring(0, 0, m))
        launch(ring(1, 0, m))
        launch(across(0, m))

    tail_row = lax.broadcasted_iota(jnp.int32, (16, 2 * ROWS), 0)
    ones = jnp.where(tail_row == 0, 1.0, 0.0).astype(BF16)
    for s in range(n):
        vbuf[s, VROWS:ACC, :] = ones
    m_ref[...] = jnp.full(m_ref.shape, FAR, F32)
    acc[...] = jnp.zeros(acc.shape, F32)

    end0 = lengths[0]
    end1 = end0 + lengths[1]
    end2 = end1 + lengths[2]

    def positions(first, second, index):
        return jnp.where(index < BLOCK, first * BLOCK + index, second * BLOCK + index - BLOCK)

    def document(pos):
        return (
            (pos >= end0).astype(jnp.int32)
            + (pos >= end1).astype(jnp.int32)
            + (pos >= end2).astype(jnp.int32)
        )

    here0, here1 = order[2 * me], order[2 * me + 1]
    down = lax.broadcasted_iota(jnp.int32, (ROWS, ROWS), 0)
    along = lax.broadcasted_iota(jnp.int32, (ROWS, ROWS), 1)
    doc_down = document(positions(here0, here1, down))
    pos_along = positions(here0, here1, along)
    doc_along = document(pos_along)
    low_along = jnp.where(
        doc_along == 0, 0, jnp.where(doc_along == 1, end0, jnp.where(doc_along == 2, end1, end2))
    )
    member_b = jnp.where(doc_down == along // FEAT, 1.0, 0.0)
    member_a = jnp.where(doc_along == down // FEAT, 1.0, 0.0)
    doc_rows[...] = member_a

    for load in loads[4:]:
        load.wait()
    for g in range(KV):
        for h in range(GROUP):
            lane = (g * GROUP + h) * HEAD
            qs[g, h * ROWS:(h + 1) * ROWS, :] = q_v[:, lane:lane + HEAD]
    def weigh():
        signs_b = (2 * us_v[...] - 1).astype(F32).astype(BF16)
        signs_b = jnp.concatenate([signs_b] * DOCS, axis=0)
        for g in range(KV):
            up_g = au_v[:, g * HEAD:(g + 1) * HEAD]
            sign_g = signs_b[:, g * HEAD:(g + 1) * HEAD]
            for h in range(GROUP):
                lane = (g * GROUP + h) * HEAD
                grad = g_v[:, lane:lane + HEAD]
                rows = slice(h * ROWS, (h + 1) * ROWS)
                a_hi, a_lo = split2(lax.dot_general(grad, up_g, NT, preferred_element_type=F32))
                b_hi, b_lo = split2(
                    lax.dot_general(grad, sign_g, NT, preferred_element_type=F32) * member_b
                )
                w_hi[g, rows, 0:RANK] = a_hi
                w_lo[g, rows, 0:RANK] = a_lo
                w_hi[g, rows, RANK:2 * RANK] = b_hi
                w_lo[g, rows, RANK:2 * RANK] = b_lo

    def chunk(*slots):
        biases = []
        for slot in slots:
            for m in range(4):
                across(slot, m).wait_recv()
            origin = device_at(lax.rem(spot + n - slot, n), 0)
            bias = []
            for which in (0, 1):
                source = origin + core * (1 - 2 * which) + which
                pos = positions(order[2 * source], order[2 * source + 1], down)
                allowed = (pos <= pos_along) & (pos >= low_along)
                bias.append(jnp.where(allowed, 0.0, FAR))
            bias = jnp.concatenate(bias, axis=0)
            biases.append(jnp.concatenate([bias] * GROUP, axis=1))

        def one(g, carry):
            before = m_ref[g]
            top = before
            scores = []
            for slot, bias in zip(slots, biases):
                keys = kbuf[slot, g].reshape(2 * ROWS, HEAD)
                part_scores = lax.dot_general(keys, qs[g], NT, preferred_element_type=F32) + bias
                scores.append(part_scores)
                top = jnp.maximum(top, jnp.max(part_scores, axis=0, keepdims=True))
            shrink = jnp.exp2((before - top) * GAIN)
            m_ref[g] = top
            total = acc[g] * shrink
            for slot, part_scores in zip(slots, scores):
                weights = jnp.exp2((part_scores - top) * GAIN).astype(BF16)
                total = total + dot(vbuf[slot], weights)
            acc[g] = total
            return carry

        lax.fori_loop(0, KV, one, 0, unroll=True)

    def pass_on(s, m):
        for way in (0, 1):
            ring(way, s - 1, m).wait_recv()
            if s < half - 1 or m % 2 == way:
                launch(ring(way, s, m))
        for slot in (s, n - s):
            launch(across(slot, m))

    pending = [0]
    for s in range(1, half):
        for m in (0, 1):
            pass_on(s, m)
        for m in (2, 3):
            pass_on(s, m)
        chunk(*pending)
        if s == 1:
            weigh()
        pending = [s, n - s]
    for m in range(4):
        ring(m % 2, half - 1, m).wait_recv()
        launch(across(half, m))
    chunk(*pending)
    chunk(half)

    raw_a = jnp.zeros((DOCS * FEAT, RANK), F32)
    raw_b = jnp.zeros((RANK, DOCS * FEAT), F32)
    for g in range(KV):
        scaled = acc[g, 0:VROWS, :] / acc[g, VROWS:VROWS + 1, :]
        left = scaled[RANK:RANK + FEAT] + scaled[RANK + FEAT:VROWS]
        left = jnp.concatenate([left] * DOCS, axis=0)
        left = left * jnp.concatenate([doc_rows[...]] * GROUP, axis=1)
        raw_a = raw_a + dot3(left, w_hi[g, :, 0:RANK], w_lo[g, :, 0:RANK])
        raw_b = raw_b + dot3(
            scaled[0:RANK], w_hi[g, :, RANK:2 * RANK], w_lo[g, :, RANK:2 * RANK]
        )
    partial[0:ROWS, :] = raw_a
    for d in range(DOCS):
        partial[ROWS + d * FEAT:ROWS + (d + 1) * FEAT, :] = jnp.concatenate(
            [raw_b[k * 32:(k + 1) * 32, d * FEAT:(d + 1) * FEAT] for k in range(4)], axis=1
        )

    piece = 2 * ROWS // n_dev

    def rows_of(device):
        return pl.ds(pl.multiple_of(device * piece, piece), piece)

    def scatter(k):
        peer = lax.rem(me + k, n_dev)
        return pltpu.make_async_remote_copy(
            src_ref=partial.at[rows_of(peer)], dst_ref=rbuf.at[k],
            send_sem=ar_send.at[0, k], recv_sem=ar_recv.at[0, k],
            device_id={"ctx": peer}, device_id_type=pl.DeviceIdType.MESH,
        )

    def spread(k):
        peer = lax.rem(me + k, n_dev)
        return pltpu.make_async_remote_copy(
            src_ref=fin.at[me], dst_ref=fin.at[me],
            send_sem=ar_send.at[1, k], recv_sem=ar_recv.at[1, k],
            device_id={"ctx": peer}, device_id_type=pl.DeviceIdType.MESH,
        )

    def arrival(k):
        source = lax.rem(me + n_dev - k, n_dev)
        return pltpu.make_async_remote_copy(
            src_ref=fin.at[source], dst_ref=fin.at[source],
            send_sem=ar_send.at[1, k], recv_sem=ar_recv.at[1, k],
            device_id={"ctx": lax.rem(me + k, n_dev)}, device_id_type=pl.DeviceIdType.MESH,
        )

    for k in range(1, n_dev):
        scatter(k).start()
    rbuf[0] = partial[rows_of(me), :]
    for copy in sent:
        copy.wait_send()
    for k in range(1, n_dev):
        scatter(k).wait_recv()
    fin[me] = jnp.sum(rbuf[...], axis=0)
    for k in range(1, n_dev):
        spread(k).start()
    for k in range(1, n_dev):
        scatter(k).wait_send()
    for k in range(1, n_dev):
        arrival(k).wait_recv()
    whole = fin[...].reshape(2 * DOCS, FEAT, RANK)
    mean = jnp.sum(
        jnp.sum(whole * whole, axis=1, keepdims=True), axis=2, keepdims=True
    ) * (1.0 / (FEAT * RANK))
    partial[...] = (whole * lax.rsqrt(mean + EPS)).reshape(2 * ROWS, RANK)
    for k in range(2):
        for f in range(FEAT):
            lane = (k * FEAT + f) * RANK
            out_ref[:, lane:lane + RANK] = partial[pl.ds(k * ROWS + f, DOCS, stride=FEAT), :]
    for k in range(1, n_dev):
        spread(k).wait_send()


def per_device(n_dev, x, q, k, g, ad, au, ds, us, order, lengths):
    n = n_dev // 2
    ds, us = ds.T, us.T
    anywhere = pl.BlockSpec(memory_space=pl.ANY)
    scalars = pl.BlockSpec(memory_space=pltpu.SMEM)
    dma = pltpu.SemaphoreType.DMA
    vmem = pltpu.VMEM
    return pl.pallas_call(
        functools.partial(kernel, n_dev),
        out_shape=jax.ShapeDtypeStruct((DOCS, 2 * FEAT * RANK), F32),
        in_specs=[anywhere] * 8 + [scalars] * 2,
        out_specs=pl.BlockSpec(memory_space=pltpu.VMEM),
        scratch_shapes=[vmem(a.shape, a.dtype) for a in (x, q, k, g, ad, au, ds, us)]
        + [
            vmem((n, KV, 2, ROWS, HEAD), BF16),
            vmem((n, ACC, 2 * ROWS), BF16),
            vmem((KV, WIDE, HEAD), BF16),
            vmem((KV, WIDE, 2 * RANK), BF16),
            vmem((KV, WIDE, 2 * RANK), BF16),
            vmem((KV, 1, WIDE), F32),
            vmem((KV, ACC, WIDE), F32),
            vmem((RANK, ROWS), F32),
            vmem((2 * ROWS, RANK), F32),
            vmem((n_dev, 2 * ROWS // n_dev, RANK), F32),
            vmem((n_dev, 2 * ROWS // n_dev, RANK), F32),
            vmem((ROWS, ROWS), F32),
            dma((8,)),
            dma((2, n // 2, 4)),
            dma((n, 4)),
            dma((n, 4)),
            dma((n, 4)),
            dma((2, n_dev)),
            dma((2, n_dev)),
        ],
        compiler_params=pltpu.CompilerParams(
            collective_id=0, has_side_effects=True, vmem_limit_bytes=60 * 1024 * 1024
        ),
    )(x, q, k, g, ad, au, ds, us, order, lengths)


def solution(mesh):
    rows = P(("groups", "ctx"), None)
    placed = (rows, rows, rows, rows, P(), P(), P(), P(), P("groups"), P("groups"))
    return jax.shard_map(
        functools.partial(per_device, mesh.shape["ctx"]),
        mesh=mesh, in_specs=placed, out_specs=P("groups", None), check_vma=False,
    )
```
